256 devices in a mesh: dp: 64 (over z, x, core), mp: 4 (over y).
Axes of the slice: x: 4, y: 4, z: 8, core: 2. Of those that a mesh axis runs over, the one named last changes fastest.
Arguments:
- queries: bfloat16 [131072, 2048], P('dp', 'mp'), may hold values from -102 to 102
- cotangent: bfloat16 [131072, 2048], P('dp', 'mp'), may hold values from -12 to 12
- passages: bfloat16 [128, 128, 4096], P('dp', None, 'mp'), may hold values from -6 to 6
- w_kv: bfloat16 [4096, 2, 2048], P(None, None, 'mp'), may hold values from -0.09375 to 0.09375
- neighbour_ids: int32 [64, 32, 2], P('dp'), may hold values from 0 to 127, as said below
- passage_slot: int32 [128], replicated, may hold values from 0 to 127, as said below
Outputs:
- grad_passages: bfloat16 [128, 128, 4096], P('dp', None, 'mp')
The draws below stay inside these ranges and needn't reach their ends.
Inputs may be any that keep to these rules, and one draw needn't show every extreme that they name: `passage_slot`: a permutation of the slots. The slots passage_slot[neighbour_ids] of the 64 neighbours of one sequence, divided by 2, take every value 0 to 63 exactly 1 times; a passage may be named more than once.
All inputs are finite; a program needn't handle non-finite values.
Results may differ from the reference program's by a relative error of at most 0.028.
The reference program's roundings to bfloat16 on the way (of `key_value`, `dscore`, `probs_low` and `grad_kv`) count: a program that leaves them out, or rounds other values in their place, can miss the bound.
Values may be sent and summed in bfloat16 or wider, within the bound.
No kernel may reach another device: no remote copies, remote signals or barrier semaphores. Data moves between devices by JAX's collectives and lax.ppermute only.
A program may use at most 192 MiB of HBM per device.

```python
import math
import jax
import jax.numpy as jnp
from jax import lax

D = 4096
HEADS = 16
HEAD_DIM = 128
GROUP = 64
NEIGH_LEN = 128
QW = 2048
GROUPS = 32
SEQ_LEN = 2048
TOKENS = 131072
ENC_DEV = 2
PASSAGES = 128
N_DP = 64


def shuffled(one_key):
    return jax.random.permutation(one_key, 2 * GROUPS)


def neighbour_tables(key):
    slot_key, owner_key, local_key = jax.random.split(key, 3)
    slot_of = jax.random.permutation(slot_key, PASSAGES).astype(jnp.int32)
    passage_at = jnp.argsort(slot_of).astype(jnp.int32)
    orders = jax.vmap(shuffled)(jax.random.split(owner_key, N_DP))
    owner_shard = (orders % N_DP).astype(jnp.int32)
    local_slot = jax.random.randint(local_key, (N_DP, 2 * GROUPS), 0, ENC_DEV).astype(jnp.int32)
    picked = passage_at[owner_shard * ENC_DEV + local_slot]
    return (slot_of, picked.reshape(N_DP, GROUPS, 2).astype(jnp.int32))


def draw_passage_slot(key, part):
    tables = neighbour_tables(key)
    return tables[0]


def draw_neighbour_ids(key, part):
    tables = neighbour_tables(key)
    return tables[1]


def draw_queries(key, part):
    key = jax.random.fold_in(key, 7)
    value_key = jax.random.fold_in(key, 0)
    return jnp.clip(jax.random.normal(value_key, (TOKENS, QW), jnp.float32), -6.0, 6.0).astype(jnp.bfloat16)


def levels(own_key, shape, pieces, low, high):
    def one(axis_at, blocks):
        draws = jax.random.uniform(jax.random.fold_in(jax.random.fold_in(own_key, 6), axis_at), (blocks,), jnp.float32, low / len(pieces), high / len(pieces))
        return jnp.repeat(jnp.exp(draws), shape[axis_at] // blocks).reshape((-1,) + (1,) * (len(shape) - axis_at - 1))

    gain = one(*pieces[0])
    for cut in pieces[1:]:
        gain = gain * one(*cut)
    return gain


def centred(rng, extent, deviation, reach, cuts=(), dtype=jnp.bfloat16):
    entries = jax.random.normal(rng, extent, jnp.float32) * deviation
    if len(cuts) > 0:
        entries = levels(rng, extent, cuts, -0.22, 0.18) * entries
    return jnp.clip(entries, min=-reach, max=reach).astype(dtype)


def setup_inputs(seed: int = 0) -> dict:
    keys = jax.random.split(jax.random.key(seed), 7)
    return {
        "queries": draw_queries(jax.random.fold_in(keys[6], 71), 0),
        "cotangent": centred(keys[1], (TOKENS, QW), 2.0, 12.0, ((0, 64), (1, 4))),
        "passages": centred(keys[2], (PASSAGES, NEIGH_LEN, D), 1.0, 6.0, ((0, 64), (2, 4))),
        "w_kv": centred(keys[3], (D, 2, QW), D ** -0.5, 0.09375, ((2, 4),)),
        "neighbour_ids": draw_neighbour_ids(jax.random.fold_in(keys[6], 71), 0),
        "passage_slot": draw_passage_slot(jax.random.fold_in(keys[6], 71), 0),
    }


def reference(queries, cotangent, passages, w_kv, neighbour_ids, passage_slot):
    kv_width = queries.shape[1]
    score_scale = 1.0 / math.sqrt(HEAD_DIM)
    key_value = jnp.einsum('pnd,dkw->pnkw', passages.astype(jnp.float32), w_kv.astype(jnp.float32)).astype(jnp.bfloat16)
    slot_rows = passage_slot[neighbour_ids]

    def one_sequence(running, inputs):
        query_seq, grad_seq, row_seq = inputs
        query_f = query_seq.astype(jnp.float32).reshape(GROUPS, GROUP, HEADS, HEAD_DIM)
        grad_out = grad_seq.astype(jnp.float32).reshape(GROUPS, GROUP, HEADS, HEAD_DIM)
        picked = key_value[row_seq.reshape(-1)].astype(jnp.float32).reshape(GROUPS, 2 * NEIGH_LEN, 2, HEADS, HEAD_DIM)
        key_rows = picked[:, :, 0]
        value_rows = picked[:, :, 1]
        scores = jnp.einsum('cqhe,ckhe->chqk', query_f, key_rows) * score_scale
        peak_score = lax.optimization_barrier(jnp.max(scores, axis=3, keepdims=True))
        log_total = peak_score + jnp.log(lax.optimization_barrier(jnp.sum(jnp.exp(scores - peak_score), axis=3, keepdims=True)))
        softmax_w = jnp.exp(scores - log_total)
        attended = jnp.einsum('chqk,ckhe->cqhe', softmax_w, value_rows)
        delta_rows = lax.optimization_barrier(jnp.sum(grad_out * attended, axis=3))
        grad_prob = jnp.einsum('cqhe,ckhe->chqk', grad_out, value_rows)
        dscore = softmax_w * (grad_prob - jnp.transpose(delta_rows, (0, 2, 1))[..., None])
        dscore = lax.optimization_barrier(dscore.astype(jnp.bfloat16)).astype(jnp.float32)
        probs_low = lax.optimization_barrier(softmax_w.astype(jnp.bfloat16)).astype(jnp.float32)
        grad_values = jnp.einsum('chqk,cqhe->ckhe', probs_low, grad_out)
        grad_keys = jnp.einsum('chqk,cqhe->ckhe', dscore, query_f) * score_scale
        grad_pair = jnp.stack([grad_keys, grad_values], axis=2).reshape(GROUPS * 2, NEIGH_LEN, 2, kv_width)
        return (running.at[row_seq.reshape(-1)].add(grad_pair), None)
    running = jnp.zeros(key_value.shape, jnp.float32)
    running, _ = lax.scan(one_sequence, running, (queries.reshape(N_DP, SEQ_LEN, kv_width), cotangent.reshape(N_DP, SEQ_LEN, kv_width), slot_rows))
    grad_kv = running.astype(jnp.bfloat16)
    return jnp.einsum('pnkw,dkw->pnd', grad_kv.astype(jnp.float32), w_kv.astype(jnp.float32)).astype(jnp.bfloat16)
```

```python
import math

import jax
import jax.numpy as jnp
from jax import lax
from jax.experimental import pallas as pl
from jax.experimental.pallas import tpu as pltpu
from jax.sharding import Mesh
from jax.sharding import PartitionSpec as P

HEAD_DIM = 128
GROUP = 64
NZ, NX, NC, NY = 8, 4, 2, 4
NLAYER = NX * NC
ENC = 2
NEAR = 128
LAYER = ("x", "c")
CHUNKS = ((0, 2), (2, 2))
BF16 = jnp.bfloat16
F32 = jnp.float32
NT = (((1,), (1,)), ((), ()))
NN = (((1,), (0,)), ((), ()))
SCALE = 1.0 / math.sqrt(HEAD_DIM)


def queue_kernel(ids, slot_of, q_ref, cot_ref, out_ref, group_at):
    dest = pl.program_id(0)

    @pl.when(dest == 0)
    def _():
        def place(ref, carry):
            group_at[slot_of[ids[ref]] // ENC] = ref // 2
            return carry

        lax.fori_loop(0, NZ * NLAYER, place, 0)

    for z in range(NZ):
        group = group_at[z * NLAYER + dest]
        out_ref[0, 0, z] = q_ref[group]
        out_ref[0, 1, z] = cot_ref[group]


def queue_groups(ids, slot_of, queries, cotangent, first, heads):
    groups = queries.shape[0]
    width = heads * HEAD_DIM
    at = first // heads
    source = pl.BlockSpec((groups, GROUP, width), lambda i, *_: (0, 0, at))
    return pl.pallas_call(
        queue_kernel,
        grid_spec=pltpu.PrefetchScalarGridSpec(
            num_scalar_prefetch=2,
            grid=(NLAYER,),
            in_specs=[source, source],
            out_specs=pl.BlockSpec((1, 2, NZ, GROUP, width), lambda i, *_: (i, 0, 0, 0, 0)),
            scratch_shapes=[pltpu.SMEM((NZ * NLAYER,), jnp.int32)],
        ),
        out_shape=jax.ShapeDtypeStruct((NLAYER, 2, NZ, GROUP, width), BF16),
        compiler_params=pltpu.CompilerParams(vmem_limit_bytes=24 * 1024 * 1024),
        cost_estimate=pl.CostEstimate(
            flops=0, bytes_accessed=3 * groups * GROUP * width * 4, transcendentals=0
        ),
        name="queue_groups",
    )(ids, slot_of, queries, cotangent)


def pick(both, second):
    return jnp.where(second, both[NEAR:], both[:NEAR])


def head_parts(visit_ref, kv_ref, head):
    cols = slice(head * HEAD_DIM, (head + 1) * HEAD_DIM)
    rows = NLAYER * GROUP
    q = visit_ref[:, 0, 0, :, cols].reshape(rows, HEAD_DIM)
    cot = visit_ref[:, 1, 0, :, cols].reshape(rows, HEAD_DIM)
    return q, cot, kv_ref[0, 0, :, cols], kv_ref[0, 1, :, cols]


def scores_of(q, cot, keys, values, second):
    score = lax.dot_general(keys, q, NT, preferred_element_type=F32)
    grad_prob = lax.dot_general(values, cot, NT, preferred_element_type=F32)
    return pick(score, second) * SCALE, pick(grad_prob, second)


def stats_kernel(heads, slot_ref, visit_ref, kv_ref, out_ref):
    z = pl.program_id(0)
    second = slot_ref[pl.ds(z, 1), :] == 1
    lse_rows, delta_rows = [], []
    for head in range(heads):
        score, grad_prob = scores_of(*head_parts(visit_ref, kv_ref, head), second)
        peak = jnp.max(score, axis=0, keepdims=True)
        weight = jnp.exp(score - peak)
        mass = jnp.sum(weight, axis=0, keepdims=True)
        lse_rows.append(peak + jnp.log(mass))
        delta_rows.append(jnp.sum(weight * grad_prob, axis=0, keepdims=True) / mass)
    for at, row in enumerate(lse_rows + delta_rows):
        out_ref[pl.ds(at * NZ + z, 1), :] = row


def visit_spec(width):
    return pl.BlockSpec((NLAYER, 2, 1, GROUP, width), lambda z, *_: (0, 0, z, 0, 0))


def kv_spec(width):
    return pl.BlockSpec((1, 2, ENC * NEAR, width), lambda z, *_: (z, 0, 0, 0))


def whole(shape):
    return pl.BlockSpec(shape, lambda z, *_: (0,) * len(shape))


def attention_cost(heads, matmuls):
    products = NZ * heads * NLAYER * GROUP * ENC * NEAR * HEAD_DIM
    moved = NZ * heads * HEAD_DIM * 2 * (2 * NLAYER * GROUP + 2 * ENC * NEAR)
    return pl.CostEstimate(
        flops=2 * matmuls * products,
        bytes_accessed=moved,
        transcendentals=NZ * heads * NLAYER * GROUP * NEAR,
    )


def partial_stats(slot_lanes, visit, kv, heads):
    width = heads * HEAD_DIM
    lanes = NLAYER * GROUP
    return pl.pallas_call(
        lambda *refs: stats_kernel(heads, *refs),
        grid=(NZ,),
        in_specs=[whole((NZ, lanes)), visit_spec(width), kv_spec(width)],
        out_specs=whole((NZ * 2 * heads, lanes)),
        out_shape=jax.ShapeDtypeStruct((NZ * 2 * heads, lanes), F32),
        compiler_params=pltpu.CompilerParams(vmem_limit_bytes=32 * 1024 * 1024),
        cost_estimate=attention_cost(heads, 2),
        name="partial_stats",
    )(slot_lanes, visit, kv)


def grads_kernel(heads, partner, slot_ref, visit_ref, kv_ref, own_ref, all_ref, out_ref):
    z = pl.program_id(0)
    second = slot_ref[pl.ds(z, 1), :] == 1
    low_lane = lax.broadcasted_iota(jnp.int32, (NZ, 2 * GROUP), 1) < GROUP
    z_row = lax.broadcasted_iota(jnp.int32, (NZ, 2 * GROUP), 0)
    places = [partner[z * NLAYER + source] for source in range(NLAYER)]

    def other(row):
        pieces = []
        for pair in range(NLAYER // 2):
            cols = slice(pair * 2 * GROUP, (pair + 1) * 2 * GROUP)
            low, high = (
                jnp.where(
                    z_row == where % NZ, all_ref[where // NZ, row * NZ : (row + 1) * NZ, cols], 0.0
                )
                for where in places[2 * pair : 2 * pair + 2]
            )
            pieces.append(jnp.sum(jnp.where(low_lane, low, high), axis=0, keepdims=True))
        return jnp.concatenate(pieces, axis=1)

    def mine(row):
        return own_ref[pl.ds(row * NZ + z, 1), :]

    totals, deltas = [], []
    for head in range(heads):
        lse_mine, lse_other = mine(head), other(head)
        top = jnp.maximum(lse_mine, lse_other)
        total = top + jnp.log(jnp.exp(lse_mine - top) + jnp.exp(lse_other - top))
        totals.append(total)
        deltas.append(
            mine(heads + head) * jnp.exp(lse_mine - total)
            + other(heads + head) * jnp.exp(lse_other - total)
        )
    for head in range(heads):
        cols = slice(head * HEAD_DIM, (head + 1) * HEAD_DIM)
        q, cot, keys, values = head_parts(visit_ref, kv_ref, head)
        score, grad_prob = scores_of(q, cot, keys, values, second)
        probs = jnp.exp(score - totals[head])
        dscore = probs * (grad_prob - deltas[head])
        for at, (weight, rows_of) in enumerate(((dscore, q), (probs, cot))):
            spread = jnp.concatenate(
                [jnp.where(second, 0.0, weight), jnp.where(second, weight, 0.0)], axis=0
            ).astype(BF16)
            grad = lax.dot_general(spread, rows_of, NN, preferred_element_type=F32)
            if at == 0:
                grad = grad * SCALE
            out_ref[0, at, :, cols] = grad.astype(BF16)


def visit_grads(partner, slot_lanes, visit, kv, own, gathered, heads):
    width = heads * HEAD_DIM
    lanes = NLAYER * GROUP
    rows = NZ * 2 * heads
    return pl.pallas_call(
        lambda *refs: grads_kernel(heads, *refs),
        grid_spec=pltpu.PrefetchScalarGridSpec(
            num_scalar_prefetch=1,
            grid=(NZ,),
            in_specs=[
                whole((NZ, lanes)),
                visit_spec(width),
                kv_spec(width),
                whole((rows, lanes)),
                whole((NLAYER, rows, lanes)),
            ],
            out_specs=kv_spec(width),
        ),
        out_shape=jax.ShapeDtypeStruct((NZ, 2, ENC * NEAR, width), BF16),
        compiler_params=pltpu.CompilerParams(vmem_limit_bytes=32 * 1024 * 1024),
        cost_estimate=attention_cost(heads, 4),
        name="visit_grads",
    )(partner, slot_lanes, visit, kv, own, gathered)


def per_device(queries, cotangent, passages, w_kv, neighbour_ids, passage_slot):
    enc_count, near_len, part_width = passages.shape
    seq_tokens, part_cols = queries.shape
    groups = seq_tokens // GROUP
    ids = neighbour_ids.reshape(-1)
    queries = queries.reshape(groups, GROUP, part_cols)
    cotangent = cotangent.reshape(groups, GROUP, part_cols)

    visits = [
        lax.all_to_all(
            queue_groups(ids, passage_slot, queries, cotangent, first, heads),
            LAYER,
            split_axis=0,
            concat_axis=0,
            tiled=True,
        )
        for first, heads in CHUNKS
    ]

    encoded = lax.all_gather(passages, "y", axis=2, tiled=True).reshape(enc_count * near_len, -1)

    layer_ids = lax.all_gather(ids, LAYER, axis=0, tiled=False)
    layer_slots = passage_slot[layer_ids]
    owner = layer_slots // ENC
    partner_owner = owner.reshape(NLAYER, groups, 2)[:, :, ::-1].reshape(NLAYER, -1)
    here = lax.axis_index("x") * NC + lax.axis_index("c")
    targets = jnp.arange(NZ, dtype=jnp.int32) * NLAYER + here
    hits = (owner[None] == targets[:, None, None]).astype(jnp.int32)
    local_slot = jnp.sum(hits * (layer_slots % ENC)[None], axis=2)
    partner = jnp.sum(hits * partner_owner[None], axis=2)
    partner = ((partner % NLAYER) * NZ + partner // NLAYER).reshape(-1)
    slot_lanes = jnp.repeat(local_slot, GROUP, axis=1)

    grads = []
    for (first, heads), visit in zip(CHUNKS, visits, strict=True):
        cols = slice(first * HEAD_DIM, (first + heads) * HEAD_DIM)
        kv_here = jnp.einsum(
            "nd,dkw->knw", encoded, w_kv[:, :, cols], preferred_element_type=F32
        ).astype(BF16)
        kv = lax.all_gather(kv_here, "z", axis=0, tiled=False)
        own = partial_stats(slot_lanes, visit, kv, heads)
        gathered = lax.all_gather(own, LAYER, axis=0, tiled=False)
        grad = visit_grads(partner, slot_lanes, visit, kv, own, gathered, heads)
        grads.append(lax.psum_scatter(grad, "z", scatter_dimension=0, tiled=False))
    grad_kv = jnp.concatenate(grads, axis=2)
    head_term = jnp.einsum("knw,dkw->nd", grad_kv, w_kv, preferred_element_type=F32).astype(BF16)
    out = lax.psum_scatter(head_term, "y", scatter_dimension=1, tiled=True)
    return out.reshape(enc_count, near_len, part_width)


def solution(mesh):
    fine = Mesh(mesh.devices.reshape(NZ, NX, NC, NY), ("z", "x", "c", "y"))
    dp = ("z", "x", "c")
    placed = (
        P(dp, "y"),
        P(dp, "y"),
        P(dp, None, "y"),
        P(None, None, "y"),
        P(dp, None, None),
        P(),
    )
    return jax.shard_map(
        per_device, mesh=fine, in_specs=placed, out_specs=P(dp, None, "y"), check_vma=False
    )
```

```python
import math

import jax
import jax.numpy as jnp
from jax import lax
from jax.experimental import pallas as pl
from jax.experimental.pallas import tpu as pltpu
from jax.sharding import Mesh
from jax.sharding import PartitionSpec as P

HEAD_DIM = 128
GROUP = 64
NZ, NX, NC, NY = 8, 4, 2, 4
NLAYER = NX * NC
ENC = 2
NEAR = 128
LAYER = ("x", "c")
HALF = NLAYER // 2
KERNEL_VMEM = 24 * 1024 * 1024
LOADS = 4
META = 2 * NZ
BF16 = jnp.bfloat16
F32 = jnp.float32
NT = (((1,), (1,)), ((), ()))
NN = (((1,), (0,)), ((), ()))
SCALE = 1.0 / math.sqrt(HEAD_DIM)
SMEM_WHOLE = pl.BlockSpec(memory_space=pltpu.SMEM)
VMEM_WHOLE = pl.BlockSpec(memory_space=pltpu.VMEM)
ANY_WHOLE = pl.BlockSpec(memory_space=pl.ANY)


def queue_kernel(
    ids, slot_of, q_hbm, cot_hbm, out_hbm, q_ref, cot_ref, meta_f32, meta_ref, load, store, meta_sem
):
    groups = q_ref.shape[0]
    part = groups // LOADS

    def loads(at):
        rows = pl.ds(at * part, part)
        return (
            pltpu.make_async_copy(q_hbm.at[rows], q_ref.at[rows], load.at[0, at]),
            pltpu.make_async_copy(cot_hbm.at[rows], cot_ref.at[rows], load.at[1, at]),
        )

    def stores(ref):
        owner = slot_of[ids[ref]] // ENC
        dest, z = owner % NLAYER, owner // NLAYER
        return [
            pltpu.make_async_copy(
                source.at[ref // 2],
                out_hbm.at[dest, pl.ds(pl.multiple_of((kind * NZ + z) * GROUP, GROUP), GROUP)],
                store.at[kind, ref],
            )
            for kind, source in enumerate((q_ref, cot_ref))
        ]

    for at in range(LOADS):
        for copy in loads(at):
            copy.start()

    def place(ref, carry):
        slot = slot_of[ids[ref]]
        owner = slot // ENC
        partner = slot_of[ids[ref + 1 - 2 * (ref % 2)]] // ENC
        row = (owner % NLAYER) * META + owner // NLAYER
        where = (partner % NLAYER) * NZ + partner // NLAYER
        meta_f32[pl.ds(row, 1), :] = jnp.full((1, HEAD_DIM), slot % ENC, jnp.int32).astype(F32)
        meta_f32[pl.ds(row + NZ, 1), :] = jnp.full((1, HEAD_DIM), where, jnp.int32).astype(F32)
        return carry

    lax.fori_loop(0, 2 * groups, place, 0)
    meta = meta_f32[...].astype(BF16).reshape(NLAYER, META, HEAD_DIM)
    for at in range(meta_ref.shape[2] // HEAD_DIM):
        meta_ref[:, :, at * HEAD_DIM : (at + 1) * HEAD_DIM] = meta
    meta_copy = pltpu.make_async_copy(
        meta_ref, out_hbm.at[:, pl.ds(2 * NZ * GROUP, META)], meta_sem
    )
    meta_copy.start()

    def send(ref, carry):
        for copy in stores(ref):
            copy.start()
        return carry

    def finish(ref, carry):
        for copy in stores(ref):
            copy.wait()
        return carry

    for at in range(LOADS):
        for copy in loads(at):
            copy.wait()
        lax.fori_loop(2 * part * at, 2 * part * (at + 1), send, 0)
    lax.fori_loop(0, 2 * groups, finish, 0)
    meta_copy.wait()


def queue_groups(ids, slot_of, queries, cotangent):
    groups, _, width = queries.shape
    rows = 2 * NZ * GROUP + META
    return pl.pallas_call(
        queue_kernel,
        in_specs=[SMEM_WHOLE] * 2 + [ANY_WHOLE] * 2,
        out_specs=ANY_WHOLE,
        out_shape=jax.ShapeDtypeStruct((NLAYER, rows, width), BF16),
        scratch_shapes=[
            pltpu.VMEM((groups, GROUP, width), BF16),
            pltpu.VMEM((groups, GROUP, width), BF16),
            pltpu.VMEM((NLAYER * META, HEAD_DIM), F32),
            pltpu.VMEM((NLAYER, META, width), BF16),
            pltpu.SemaphoreType.DMA((2, LOADS)),
            pltpu.SemaphoreType.DMA((2, 2 * groups)),
            pltpu.SemaphoreType.DMA,
        ],
        compiler_params=pltpu.CompilerParams(vmem_limit_bytes=60 * 1024 * 1024),
        cost_estimate=pl.CostEstimate(
            flops=0, bytes_accessed=12 * groups * GROUP * width, transcendentals=0
        ),
        name="queue_groups",
    )(ids, slot_of, queries, cotangent)


def block_copies(visit_hbm, kv_hbm, rows_ref, table_ref, sems, at, z, off):
    for kind in range(2):
        rows = pl.ds(pl.multiple_of((kind * NZ + z) * GROUP, GROUP), GROUP)
        yield pltpu.make_async_copy(
            visit_hbm.at[:, rows], rows_ref.at[at, kind], sems.at[at, kind]
        )
    yield pltpu.make_async_copy(kv_hbm.at[off], table_ref.at[at], sems.at[at, 2])


def block_scratch(count, width):
    return [
        pltpu.VMEM((count, 2, NLAYER, GROUP, width), BF16),
        pltpu.VMEM((count, 2, ENC * NEAR, width), BF16),
        pltpu.VMEM((NLAYER, META, HEAD_DIM), BF16),
        pltpu.SemaphoreType.DMA((count, 3)),
        pltpu.SemaphoreType.DMA,
    ]


def meta_copy(visit_hbm, meta_ref, sem):
    rows = pl.ds(2 * NZ * GROUP, META)
    return pltpu.make_async_copy(visit_hbm.at[:, rows, pl.ds(0, HEAD_DIM)], meta_ref, sem)


def head_operands(rows_ref, table_ref, meta_ref, at, z, head, half):
    cols = slice(head * HEAD_DIM, (head + 1) * HEAD_DIM)
    tables = [
        jnp.concatenate(
            [table_ref[at, kind, :NEAR, cols], table_ref[at, kind, NEAR:, cols]], axis=1
        )
        for kind in range(2)
    ]
    own_row = lax.broadcasted_iota(jnp.int32, (META, HEAD_DIM), 0) == z
    seconds = []
    for source in range(half * HALF, (half + 1) * HALF):
        meta = meta_ref[source].astype(F32)
        slot = jnp.sum(jnp.where(own_row, meta, 0.0), axis=0, keepdims=True)
        seconds.append(jnp.broadcast_to(slot, (GROUP, HEAD_DIM)).astype(BF16) > 0.5)
    rows = []
    for kind in range(2):
        pieces = []
        for source, second in enumerate(seconds):
            row = rows_ref[at, kind, half * HALF + source, :, cols]
            zero = jnp.zeros_like(row)
            pieces.append(
                jnp.concatenate([jnp.where(second, zero, row), jnp.where(second, row, zero)], axis=1)
            )
        rows.append(jnp.concatenate(pieces, axis=0))
    score = lax.dot_general(tables[0], rows[0], NT, preferred_element_type=F32) * SCALE
    grad_prob = lax.dot_general(tables[1], rows[1], NT, preferred_element_type=F32)
    return score, grad_prob, rows


def stats_kernel(heads, my_z, visit_hbm, kv_hbm, out_ref, rows_ref, table_ref, meta_ref, sems, sem):
    def copies(z):
        off = (z + NZ - my_z[0]) % NZ
        return block_copies(visit_hbm, kv_hbm, rows_ref, table_ref, sems, z, z, off)

    meta_copy(visit_hbm, meta_ref, sem).start()
    for z in range(NZ):
        for copy in copies(z):
            copy.start()
    meta_copy(visit_hbm, meta_ref, sem).wait()

    def one(z, carry):
        for copy in copies(z):
            copy.wait()
        for head in range(heads):
            for half in range(2):
                lanes = slice(half * HALF * GROUP, (half + 1) * HALF * GROUP)
                score, grad_prob, _ = head_operands(
                    rows_ref, table_ref, meta_ref, z, z, head, half
                )
                peak = jnp.max(score, axis=0, keepdims=True)
                weight = jnp.exp(score - peak)
                mass = jnp.sum(weight, axis=0, keepdims=True)
                delta = jnp.sum(weight * grad_prob, axis=0, keepdims=True) / mass
                out_ref[pl.ds(head * NZ + z, 1), lanes] = peak + jnp.log(mass)
                out_ref[pl.ds((heads + head) * NZ + z, 1), lanes] = delta
        return carry

    lax.fori_loop(0, NZ, one, 0)


def attention_cost(blocks, heads, matmuls):
    products = blocks * heads * NLAYER * GROUP * ENC * NEAR * HEAD_DIM
    moved = blocks * heads * HEAD_DIM * 2 * (2 * NLAYER * GROUP + 2 * ENC * NEAR)
    return pl.CostEstimate(
        flops=2 * matmuls * products,
        bytes_accessed=moved,
        transcendentals=blocks * heads * NLAYER * GROUP * NEAR,
    )


def in_hbm(array):
    return pltpu.with_memory_space_constraint(array, pltpu.HBM)


def partial_stats(my_z, visit, kv, heads):
    return pl.pallas_call(
        lambda *refs: stats_kernel(heads, *refs),
        in_specs=[SMEM_WHOLE, ANY_WHOLE, ANY_WHOLE],
        out_specs=VMEM_WHOLE,
        out_shape=jax.ShapeDtypeStruct((NZ * 2 * heads, NLAYER * GROUP), F32),
        scratch_shapes=block_scratch(NZ, heads * HEAD_DIM),
        compiler_params=pltpu.CompilerParams(vmem_limit_bytes=KERNEL_VMEM),
        cost_estimate=attention_cost(NZ, heads, 2),
        name="partial_stats",
    )(my_z, in_hbm(visit), in_hbm(kv))


def grads_kernel(heads, offsets, my_z, partner, visit_hbm, kv_hbm, own_ref, same_ref, other_ref, *refs):
    *out_refs, rows_ref, table_ref, meta_ref, sems, sem = refs

    def copies(at):
        off = offsets[at]
        z = (my_z[0] + off) % NZ
        return block_copies(visit_hbm, kv_hbm, rows_ref, table_ref, sems, at, z, off)

    meta_copy(visit_hbm, meta_ref, sem).start()
    for at in range(len(offsets)):
        for copy in copies(at):
            copy.start()
    meta_copy(visit_hbm, meta_ref, sem).wait()
    low_lane = lax.broadcasted_iota(jnp.int32, (NZ, 2 * GROUP), 1) < GROUP
    z_row = lax.broadcasted_iota(jnp.int32, (NZ, 2 * GROUP), 0)
    for at_offset, off in enumerate(offsets):
        for copy in copies(at_offset):
            copy.wait()
        z = (my_z[0] + off) % NZ
        places = [partner[source * NZ + z] for source in range(NLAYER)]

        def other(row, half, places=places):
            tiles = slice(row * NZ, (row + 1) * NZ)
            pieces = []
            for pair in range(half * HALF // 2, (half + 1) * HALF // 2):
                cols = slice(pair * 2 * GROUP, (pair + 1) * 2 * GROUP)
                low, high = (
                    jnp.where(
                        z_row == where % NZ,
                        jnp.where(
                            where < NX * NZ,
                            same_ref[(where // NZ) % NX, tiles, cols],
                            other_ref[(where // NZ) % NX, tiles, cols],
                        ),
                        0.0,
                    )
                    for where in places[2 * pair : 2 * pair + 2]
                )
                pieces.append(jnp.sum(jnp.where(low_lane, low, high), axis=0, keepdims=True))
            return jnp.concatenate(pieces, axis=1)

        for head in range(heads):
            cols = slice(head * HEAD_DIM, (head + 1) * HEAD_DIM)
            grads = [None, None]
            for half in range(2):
                lanes = slice(half * HALF * GROUP, (half + 1) * HALF * GROUP)
                score, grad_prob, rows = head_operands(
                    rows_ref, table_ref, meta_ref, at_offset, z, head, half
                )
                lse_mine = own_ref[pl.ds(head * NZ + z, 1), lanes]
                delta_mine = own_ref[pl.ds((heads + head) * NZ + z, 1), lanes]
                lse_other, delta_other = other(head, half), other(heads + head, half)
                top = jnp.maximum(lse_mine, lse_other)
                total = top + jnp.log(jnp.exp(lse_mine - top) + jnp.exp(lse_other - top))
                delta = delta_mine * jnp.exp(lse_mine - total) + delta_other * jnp.exp(
                    lse_other - total
                )
                probs = jnp.exp(score - total)
                dscore = probs * (grad_prob - delta)
                for at, weight in enumerate((dscore, probs)):
                    grad = lax.dot_general(
                        weight.astype(BF16), rows[at], NN, preferred_element_type=F32
                    )
                    grads[at] = grad if half == 0 else grads[at] + grad
            for at, grad in enumerate((grads[0] * SCALE, grads[1])):
                for slot in range(ENC):
                    part = grad[:, slot * HEAD_DIM : (slot + 1) * HEAD_DIM].astype(BF16)
                    if len(offsets) == 1:
                        out_refs[2 * slot + at][:, cols] = part
                    else:
                        out_refs[ENC * at_offset + slot][at, :, cols] = part


def visit_grads(offsets, my_z, partner, visit, kv, own, same, other, heads):
    shape = (NEAR, heads * HEAD_DIM) if len(offsets) == 1 else (2, NEAR, heads * HEAD_DIM)
    parts = 2 * ENC if len(offsets) == 1 else ENC * len(offsets)
    return pl.pallas_call(
        lambda *refs: grads_kernel(heads, offsets, *refs),
        in_specs=[SMEM_WHOLE] * 2 + [ANY_WHOLE] * 2 + [VMEM_WHOLE] * 3,
        out_specs=[VMEM_WHOLE] * parts,
        out_shape=[jax.ShapeDtypeStruct(shape, BF16)] * parts,
        scratch_shapes=block_scratch(len(offsets), heads * HEAD_DIM),
        compiler_params=pltpu.CompilerParams(vmem_limit_bytes=KERNEL_VMEM),
        cost_estimate=attention_cost(len(offsets), heads, 4),
        name="visit_grads",
    )(my_z, partner, in_hbm(visit), in_hbm(kv), own, same, other)


def shifted(array, axis, size, by):
    return lax.ppermute(array, axis, [(i, (i + by) % size) for i in range(size)])


def ring_sum(term, axis, size, add):
    far = term(size // 2)
    half = far.shape[0] // 2
    up, down = far[:half], far[half:]
    for k in range(size // 2, 0, -1):
        up = shifted(up, axis, size, 1)
        down = shifted(down, axis, size, -1)
        if k == 1:
            return add(term(0), up, down)
        above, below = term(k - 1), term(size - k + 1)
        if k == size // 2:
            up = jnp.concatenate([add(above[:half], up), above[half:]], axis=0)
            down = jnp.concatenate([below[:half], add(below[half:], down)], axis=0)
        else:
            up, down = add(above, up), add(below, down)


def add_terms(*terms):
    return sum(t.astype(F32) for t in terms).astype(BF16)


def gather_z(piece):
    below, above = [piece], [piece]
    for _ in range(NZ // 2 - 1):
        below.append(shifted(below[-1], "z", NZ, 1))
        above.append(shifted(above[-1], "z", NZ, -1))
    half = piece.shape[0] // 2
    far = [shifted(below[-1][:half], "z", NZ, 1), shifted(above[-1][half:], "z", NZ, -1)]
    return jnp.stack([*above, jnp.concatenate(far, axis=0), *below[:0:-1]])


def per_device(queries, cotangent, passages, w_kv, neighbour_ids, passage_slot):
    enc_count, near_len, part_width = passages.shape
    seq_tokens, part_cols = queries.shape
    groups = seq_tokens // GROUP
    heads = part_cols // HEAD_DIM
    my_y, my_z = lax.axis_index("y"), lax.axis_index("z")
    ids = neighbour_ids.reshape(-1)
    queries = queries.reshape(groups, GROUP, part_cols)
    cotangent = cotangent.reshape(groups, GROUP, part_cols)

    piece = passages.reshape(enc_count * near_len, part_width)
    half = piece.shape[0] // 2
    below, above = shifted(piece, "y", NY, 1), shifted(piece, "y", NY, -1)
    queued = queue_groups(ids, passage_slot, queries, cotangent)
    queued, below = lax.optimization_barrier((queued, below))
    visit = lax.all_to_all(queued, LAYER, split_axis=0, concat_axis=0, tiled=True)
    far = (shifted(below[:half], "y", NY, 1), shifted(above[half:], "y", NY, -1))

    encoded = jnp.zeros((enc_count * near_len, NY * part_width), BF16)
    for k, at, part in ((0, 0, piece), (1, 0, above), (3, 0, below), (2, 0, far[0]), (2, half, far[1])):
        encoded = lax.dynamic_update_slice(encoded, part, (at, ((my_y + k) % NY) * part_width))
    kv_here = jnp.einsum("nd,dkw->knw", encoded, w_kv, preferred_element_type=F32).astype(BF16)
    kv_here, later_w = lax.optimization_barrier((kv_here, w_kv))
    kv = gather_z(kv_here)
    weights = [
        lax.dynamic_slice_in_dim(later_w, ((my_y + k) % NY) * part_width, part_width, axis=0)
        for k in range(NY)
    ]

    visit, kv, weights = lax.optimization_barrier((visit, kv, weights))
    place = visit[:, 2 * NZ * GROUP + NZ :, 0].astype(jnp.int32)
    spot, at_z = place // NZ, place % NZ
    spot_x = (spot // NC - lax.axis_index("x")) % NX
    spot_c = (spot % NC) ^ lax.axis_index("c")
    partner = ((spot_c * NX + spot_x) * NZ + at_z).reshape(-1)
    my_z = my_z.reshape(1)
    own = partial_stats(my_z, visit, kv, heads)
    same_core = jnp.stack([own] + [shifted(own, "x", NX, -k) for k in range(1, NX)])
    other_core = shifted(same_core, "c", NC, 1)

    def z_terms(*offsets, after=()):
        at, _ = lax.optimization_barrier((my_z, after))
        return visit_grads(offsets, at, partner, visit, kv, own, same_core, other_core, heads)

    far = z_terms(4)
    ups, downs = list(far[0::2]), list(far[1::2])
    for offsets in ((3, 5), (2, 6), (1, 7, 0)):
        terms = z_terms(*offsets, after=(ups, downs) if offsets[0] < 3 else ())
        ups = [shifted(up, "z", NZ, 1) for up in ups]
        downs = [shifted(down, "z", NZ, -1) for down in downs]
        for slot in range(ENC):
            above, below = terms[slot], terms[ENC + slot]
            if offsets[0] == 3:
                ups[slot] = jnp.stack([add_terms(above[0], ups[slot]), above[1]])
                downs[slot] = jnp.stack([below[0], add_terms(below[1], downs[slot])])
            else:
                ups[slot] = add_terms(above, ups[slot])
                downs[slot] = add_terms(below, downs[slot])

    grads = []
    for slot in range(ENC):
        up, down = shifted(ups[slot], "z", NZ, 1), shifted(downs[slot], "z", NZ, -1)
        grads.append(add_terms(terms[2 * ENC + slot], up, down))
    grad_kv = jnp.concatenate(grads, axis=1)

    def y_term(k):
        return jnp.einsum(
            "knw,dkw->nd", grad_kv, weights[k], preferred_element_type=F32
        ).astype(BF16)

    out = ring_sum(y_term, "y", NY, add_terms)
    return out.reshape(enc_count, near_len, part_width)


def solution(mesh):
    fine = Mesh(mesh.devices.reshape(NZ, NX, NC, NY), ("z", "x", "c", "y"))
    dp = ("z", "x", "c")
    placed = (
        P(dp, "y"),
        P(dp, "y"),
        P(dp, None, "y"),
        P(None, None, "y"),
        P(dp, None, None),
        P(),
    )
    return jax.shard_map(
        per_device, mesh=fine, in_specs=placed, out_specs=P(dp, None, "y"), check_vma=False
    )
```

```python
import math

import jax
import jax.numpy as jnp
from jax import lax
from jax.experimental import pallas as pl
from jax.experimental.pallas import tpu as pltpu
from jax.sharding import Mesh
from jax.sharding import PartitionSpec as P

HEAD_DIM = 128
GROUP = 64
NZ, NX, NC, NY = 8, 4, 2, 4
NLAYER = NX * NC
ENC = 2
NEAR = 128
LAYER = ("x", "c")
HALF = NLAYER // 2
KERNEL_VMEM = 24 * 1024 * 1024
LOADS = 4
AHEAD = 2
HOLD = 2
FIRST_HEADS = 3
SPLIT = FIRST_HEADS * HEAD_DIM
META = 2 * NZ
BF16 = jnp.bfloat16
F32 = jnp.float32
NT = (((1,), (1,)), ((), ()))
NN = (((1,), (0,)), ((), ()))
SCALE = 1.0 / math.sqrt(HEAD_DIM)
SMEM_WHOLE = pl.BlockSpec(memory_space=pltpu.SMEM)
VMEM_WHOLE = pl.BlockSpec(memory_space=pltpu.VMEM)
ANY_WHOLE = pl.BlockSpec(memory_space=pl.ANY)


def queue_kernel(ids, slot_of, q_hbm, cot_hbm, *refs, with_meta):
    if with_meta:
        out_hbm, q_ref, cot_ref, meta_f32, meta_ref, load, store, meta_sem = refs
        first = 0
    else:
        here, same_hbm, other_hbm, q_ref, cot_ref, load, store = refs
        first = SPLIT
    groups, _, width = q_ref.shape
    part = groups // LOADS

    def loads(at):
        rows, cols = pl.ds(at * part, part), pl.ds(first, width)
        return (
            pltpu.make_async_copy(q_hbm.at[rows, :, cols], q_ref.at[rows], load.at[0, at]),
            pltpu.make_async_copy(cot_hbm.at[rows, :, cols], cot_ref.at[rows], load.at[1, at]),
        )

    def stores(ref, target, dest, z):
        for kind, source in enumerate((q_ref, cot_ref)):
            rows = pl.ds(pl.multiple_of((kind * NZ + z) * GROUP, GROUP), GROUP)
            yield pltpu.make_async_copy(
                source.at[ref // 2], target.at[dest, rows], store.at[kind, ref]
            )

    for at in range(LOADS):
        for copy in loads(at):
            copy.start()

    if with_meta:

        def place(ref, carry):
            slot = slot_of[ids[ref]]
            owner = slot // ENC
            partner = slot_of[ids[ref + 1 - 2 * (ref % 2)]] // ENC
            row = (owner % NLAYER) * META + owner // NLAYER
            where = (partner % NLAYER) * NZ + partner // NLAYER
            meta_f32[pl.ds(row, 1), :] = jnp.full((1, HEAD_DIM), slot % ENC, jnp.int32).astype(F32)
            meta_f32[pl.ds(row + NZ, 1), :] = jnp.full((1, HEAD_DIM), where, jnp.int32).astype(F32)
            return carry

        lax.fori_loop(0, 2 * groups, place, 0)
        meta = meta_f32[...].astype(BF16).reshape(NLAYER, META, HEAD_DIM)
        for at in range(width // HEAD_DIM):
            meta_ref[:, :, at * HEAD_DIM : (at + 1) * HEAD_DIM] = meta
        meta_rows = pl.ds(2 * NZ * GROUP, META)
        meta_out = pltpu.make_async_copy(meta_ref, out_hbm.at[:, meta_rows], meta_sem)
        meta_out.start()

    def send(ref, carry):
        owner = slot_of[ids[ref]] // ENC
        dest, z = owner % NLAYER, owner // NLAYER
        if with_meta:
            for copy in stores(ref, out_hbm, dest, z):
                copy.start()
            return carry
        up = (dest // NC - here[1] + NX) % NX
        own_core = dest % NC == here[2]

        @pl.when(own_core)
        def _():
            for copy in stores(ref, same_hbm, up, z):
                copy.start()

        @pl.when(jnp.logical_not(own_core))
        def _():
            for copy in stores(ref, other_hbm, up, z):
                copy.start()

        return carry

    def finish(ref, carry):
        for copy in stores(ref, out_hbm if with_meta else same_hbm, 0, 0):
            copy.wait()
        return carry

    for at in range(LOADS):
        for copy in loads(at):
            copy.wait()
        lax.fori_loop(2 * part * at, 2 * part * (at + 1), send, 0)
    lax.fori_loop(0, 2 * groups, finish, 0)
    if with_meta:
        meta_out.wait()


def queue_groups(ids, slot_of, queries, cotangent, here=None):
    with_meta = here is None
    extra = [] if with_meta else [here]
    groups, _, width = queries.shape
    width = SPLIT if with_meta else width - SPLIT
    rows = 2 * NZ * GROUP
    rest = jax.ShapeDtypeStruct((NX, rows, width), BF16)
    block = pltpu.VMEM((groups, GROUP, width), BF16)
    sems = [pltpu.SemaphoreType.DMA((2, LOADS)), pltpu.SemaphoreType.DMA((2, 2 * groups))]
    if with_meta:
        outs = [jax.ShapeDtypeStruct((NLAYER, rows + META, width), BF16)]
        meta = [
            pltpu.VMEM((NLAYER * META, HEAD_DIM), F32),
            pltpu.VMEM((NLAYER, META, width), BF16),
        ]
        sems.append(pltpu.SemaphoreType.DMA)
    else:
        outs, meta = [rest, rest], []

    def kernel(*refs):
        queue_kernel(*refs, with_meta=with_meta)

    return pl.pallas_call(
        kernel,
        in_specs=[SMEM_WHOLE] * 2 + [ANY_WHOLE] * 2 + [SMEM_WHOLE] * len(extra),
        out_specs=[ANY_WHOLE] * len(outs),
        out_shape=outs,
        scratch_shapes=[block, block, *meta, *sems],
        compiler_params=pltpu.CompilerParams(vmem_limit_bytes=60 * 1024 * 1024),
        cost_estimate=pl.CostEstimate(
            flops=0, bytes_accessed=12 * groups * GROUP * width, transcendentals=0
        ),
        name="queue_groups",
    )(ids, slot_of, queries, cotangent, *extra)


def block_copies(sources, rows_ref, rest_ref, table_ref, sems, at, z, off, head_range):
    visit_hbm, *rest_hbm, kv_hbm = sources
    first, last = head_range[0] * HEAD_DIM, head_range[1] * HEAD_DIM
    for kind in range(2):
        rows = pl.ds(pl.multiple_of((kind * NZ + z) * GROUP, GROUP), GROUP)
        if first < SPLIT:
            yield pltpu.make_async_copy(
                visit_hbm.at[:, rows], rows_ref.at[at, kind], sems.at[at, kind]
            )
            if last > SPLIT:
                for down in range(NX):
                    yield pltpu.make_async_copy(
                        rest_hbm[down].at[:, rows],
                        rest_ref.at[down, :, at, kind],
                        sems.at[at, 3 + kind * NX + down],
                    )
    yield pltpu.make_async_copy(
        kv_hbm.at[off, :, :, pl.ds(first, last - first)], table_ref.at[at], sems.at[at, 2]
    )


def block_scratch(count, head_range):
    first, last = head_range[0] * HEAD_DIM, head_range[1] * HEAD_DIM
    rest = (NX, NC, count, 2, GROUP, last - SPLIT)
    if first >= SPLIT:
        rest = (NX, NC, 2 * NZ * GROUP, last - SPLIT)
    rest = [] if last <= SPLIT else [pltpu.VMEM(rest, BF16)]
    rows = [] if first >= SPLIT else [pltpu.VMEM((count, 2, NLAYER, GROUP, SPLIT), BF16)]
    return [
        *rows,
        *rest,
        pltpu.VMEM((count, 2, ENC * NEAR, last - first), BF16),
        pltpu.VMEM((NLAYER, META, HEAD_DIM), BF16),
        pltpu.SemaphoreType.DMA((count, 3 + 2 * NX)),
        pltpu.SemaphoreType.DMA((1 + NX,)),
    ]


def meta_copy(visit_hbm, meta_ref, sem):
    rows = pl.ds(2 * NZ * GROUP, META)
    return pltpu.make_async_copy(visit_hbm.at[:, rows, pl.ds(0, HEAD_DIM)], meta_ref, sem)


def head_operands(row_of, table_ref, meta_ref, at, z, head, half):
    cols = slice(head * HEAD_DIM, (head + 1) * HEAD_DIM)
    tables = [
        jnp.concatenate(
            [table_ref[at, kind, :NEAR, cols], table_ref[at, kind, NEAR:, cols]], axis=1
        )
        for kind in range(2)
    ]
    own_row = lax.broadcasted_iota(jnp.int32, (META, HEAD_DIM), 0) == z
    seconds = []
    for source in range(half * HALF, (half + 1) * HALF):
        meta = meta_ref[source].astype(F32)
        slot = jnp.sum(jnp.where(own_row, meta, 0.0), axis=0, keepdims=True)
        seconds.append(jnp.broadcast_to(slot, (GROUP, HEAD_DIM)).astype(BF16) > 0.5)
    rows = []
    for kind in range(2):
        pieces = []
        for source, second in enumerate(seconds):
            row = row_of(kind, half * HALF + source, cols)
            zero = jnp.zeros_like(row)
            pieces.append(
                jnp.concatenate([jnp.where(second, zero, row), jnp.where(second, row, zero)], axis=1)
            )
        rows.append(jnp.concatenate(pieces, axis=0))
    score = lax.dot_general(tables[0], rows[0], NT, preferred_element_type=F32) * SCALE
    grad_prob = lax.dot_general(tables[1], rows[1], NT, preferred_element_type=F32)
    return score, grad_prob, rows


def rest_place(here, source):
    return (here[1] - source // NC + NX) % NX, (here[2] + source) % NC


def stats_kernel(head_range, here, *refs):
    *sources, out_ref, block_ref, table_ref, meta_ref, sems, sem = refs
    visit_hbm = sources[0]
    heads = head_range[1] - head_range[0]
    alone = head_range[0] * HEAD_DIM >= SPLIT
    rest_copies = []
    if alone:
        rest_copies = [
            pltpu.make_async_copy(sources[1 + down], block_ref.at[down], sem.at[1 + down])
            for down in range(NX)
        ]

    def copies(z):
        off = (z + NZ - here[0]) % NZ
        return block_copies(
            sources, block_ref, None, table_ref, sems, z, z, off, head_range
        )

    meta_copy(visit_hbm, meta_ref, sem.at[0]).start()
    for copy in rest_copies:
        copy.start()
    for z in range(NZ if alone else AHEAD):
        for copy in copies(z):
            copy.start()
    meta_copy(visit_hbm, meta_ref, sem.at[0]).wait()
    for copy in rest_copies:
        copy.wait()
    if alone:
        for z in range(NZ):
            for copy in copies(z):
                copy.wait()

    def one(z, carry):
        if not alone:

            @pl.when(z + AHEAD < NZ)
            def _():
                for copy in copies(z + AHEAD):
                    copy.start()

            for copy in copies(z):
                copy.wait()

        def row_of(kind, source, cols):
            if alone:
                down, core = rest_place(here, source)
                rows = pl.ds(pl.multiple_of((kind * NZ + z) * GROUP, GROUP), GROUP)
                return block_ref[down, core, rows, cols]
            return block_ref[z, kind, source, :, cols]

        for head in range(heads):
            for half in range(2):
                lanes = slice(half * HALF * GROUP, (half + 1) * HALF * GROUP)
                score, grad_prob, _ = head_operands(
                    row_of, table_ref, meta_ref, z, z, head, half
                )
                peak = jnp.max(score, axis=0, keepdims=True)
                weight = jnp.exp(score - peak)
                mass = jnp.sum(weight, axis=0, keepdims=True)
                delta = jnp.sum(weight * grad_prob, axis=0, keepdims=True) / mass
                out_ref[pl.ds(head * NZ + z, 1), lanes] = peak + jnp.log(mass)
                out_ref[pl.ds((heads + head) * NZ + z, 1), lanes] = delta
        return carry

    lax.fori_loop(0, NZ, one, 0, unroll=4 if alone else 1)


def attention_cost(blocks, heads, matmuls):
    products = blocks * heads * NLAYER * GROUP * ENC * NEAR * HEAD_DIM
    moved = blocks * heads * HEAD_DIM * 2 * (2 * NLAYER * GROUP + 2 * ENC * NEAR)
    return pl.CostEstimate(
        flops=2 * matmuls * products,
        bytes_accessed=moved,
        transcendentals=blocks * heads * NLAYER * GROUP * NEAR,
    )


def in_hbm(array):
    return pltpu.with_memory_space_constraint(array, pltpu.HBM)


def partial_stats(here, sources, head_range):
    heads = head_range[1] - head_range[0]
    return pl.pallas_call(
        lambda *refs: stats_kernel(head_range, *refs),
        in_specs=[SMEM_WHOLE] + [ANY_WHOLE] * len(sources),
        out_specs=VMEM_WHOLE,
        out_shape=jax.ShapeDtypeStruct((NZ * 2 * heads, NLAYER * GROUP), F32),
        scratch_shapes=block_scratch(NZ, head_range),
        compiler_params=pltpu.CompilerParams(vmem_limit_bytes=KERNEL_VMEM),
        cost_estimate=attention_cost(NZ, heads, 2),
        name="partial_stats",
    )(here, *(in_hbm(source) for source in sources))


def grads_kernel(head_ranges, offsets, here, partner, *refs):
    *sources, partials, out_refs, rows_ref, rest_ref, table_ref, meta_ref, sems, sem = refs
    visit_hbm = sources[0]
    all_heads = (0, head_ranges[-1][1])

    def copies(at):
        off = offsets[at]
        z = (here[0] + off) % NZ
        return block_copies(
            sources, rows_ref, rest_ref, table_ref, sems, at, z, off, all_heads
        )

    for copy in copies(0):
        copy.start()
    meta_copy(visit_hbm, meta_ref, sem.at[0]).start()
    meta_copy(visit_hbm, meta_ref, sem.at[0]).wait()
    low_lane = lax.broadcasted_iota(jnp.int32, (NZ, 2 * GROUP), 1) < GROUP
    z_row = lax.broadcasted_iota(jnp.int32, (NZ, 2 * GROUP), 0)
    for at_offset, off in enumerate(offsets):
        for copy in copies(at_offset):
            copy.wait()
        if at_offset + 1 < len(offsets):
            for copy in copies(at_offset + 1):
                copy.start()
        z = (here[0] + off) % NZ
        places = [partner[source * NZ + z] for source in range(NLAYER)]

        def other(same_ref, other_ref, row, half, places=places):
            tiles = slice(row * NZ, (row + 1) * NZ)
            pieces = []
            for pair in range(half * HALF // 2, (half + 1) * HALF // 2):
                cols = slice(pair * 2 * GROUP, (pair + 1) * 2 * GROUP)
                low, high = (
                    jnp.where(
                        z_row == where % NZ,
                        jnp.where(
                            where < NX * NZ,
                            same_ref[(where // NZ) % NX, tiles, cols],
                            other_ref[(where // NZ) % NX, tiles, cols],
                        ),
                        0.0,
                    )
                    for where in places[2 * pair : 2 * pair + 2]
                )
                pieces.append(jnp.sum(jnp.where(low_lane, low, high), axis=0, keepdims=True))
            return jnp.concatenate(pieces, axis=1)

        def row_of(kind, source, cols, at_offset=at_offset):
            if cols.start < SPLIT:
                return rows_ref[at_offset, kind, source, :, cols]
            down, core = rest_place(here, source)
            cols = slice(cols.start - SPLIT, cols.stop - SPLIT)
            return rest_ref[down, core, at_offset, kind, :, cols]

        for head in range(all_heads[1]):
            cols = slice(head * HEAD_DIM, (head + 1) * HEAD_DIM)
            chunk = 0 if head < head_ranges[0][1] else 1
            own_ref, *exchanged = partials[chunk]
            first, last = head_ranges[chunk]
            lse_at, delta_at = head - first, last - first + head - first
            grads = [None, None]
            for half in range(2):
                lanes = slice(half * HALF * GROUP, (half + 1) * HALF * GROUP)
                score, grad_prob, rows = head_operands(
                    row_of, table_ref, meta_ref, at_offset, z, head, half
                )
                lse_mine = own_ref[pl.ds(lse_at * NZ + z, 1), lanes]
                delta_mine = own_ref[pl.ds(delta_at * NZ + z, 1), lanes]
                lse_other = other(*exchanged, lse_at, half)
                delta_other = other(*exchanged, delta_at, half)
                top = jnp.maximum(lse_mine, lse_other)
                total = top + jnp.log(jnp.exp(lse_mine - top) + jnp.exp(lse_other - top))
                delta = delta_mine * jnp.exp(lse_mine - total) + delta_other * jnp.exp(
                    lse_other - total
                )
                probs = jnp.exp(score - total)
                dscore = probs * (grad_prob - delta)
                for at, weight in enumerate((dscore, probs)):
                    grad = lax.dot_general(
                        weight.astype(BF16), rows[at], NN, preferred_element_type=F32
                    )
                    grads[at] = grad if half == 0 else grads[at] + grad
            for at, grad in enumerate((grads[0] * SCALE, grads[1])):
                for slot in range(ENC):
                    part = grad[:, slot * HEAD_DIM : (slot + 1) * HEAD_DIM].astype(BF16)
                    if len(offsets) == 1:
                        out_refs[at][slot, :, cols] = part
                    else:
                        out_refs[ENC * at_offset + slot][at, :, cols] = part


def visit_grads(offsets, here, partner, sources, partials, head_ranges):
    width = head_ranges[-1][1] * HEAD_DIM
    parts = 2 * len(offsets)
    count = len(sources)
    flat = [array for chunk in partials for array in chunk]

    def kernel(here, partner, *refs):
        refs = list(refs)
        ins, refs = refs[:count], refs[count:]
        chunks, refs = refs[: len(flat)], refs[len(flat) :]
        chunks = [chunks[3 * i : 3 * i + 3] for i in range(len(head_ranges))]
        grads_kernel(head_ranges, offsets, here, partner, *ins, chunks, refs[:parts], *refs[parts:])

    return pl.pallas_call(
        kernel,
        in_specs=[SMEM_WHOLE] * 2 + [ANY_WHOLE] * count + [VMEM_WHOLE] * len(flat),
        out_specs=[VMEM_WHOLE] * parts,
        out_shape=[jax.ShapeDtypeStruct((2, NEAR, width), BF16)] * parts,
        scratch_shapes=block_scratch(len(offsets), (0, head_ranges[-1][1])),
        compiler_params=pltpu.CompilerParams(vmem_limit_bytes=KERNEL_VMEM),
        cost_estimate=attention_cost(len(offsets), width // HEAD_DIM, 4),
        name="visit_grads",
    )(here, partner, *(in_hbm(source) for source in sources), *flat)


def shifted(array, axis, size, by):
    return lax.ppermute(array, axis, [(i, (i + by) % size) for i in range(size)])


def ring_sum(term, axis, size, add):
    far = term(size // 2)
    half = far.shape[0] // 2
    up, down = far[:half], far[half:]
    for k in range(size // 2, 0, -1):
        up = shifted(up, axis, size, 1)
        down = shifted(down, axis, size, -1)
        if k == 1:
            return add(term(0), up, down)
        above, below = term(k - 1), term(size - k + 1)
        if k == size // 2:
            up = jnp.concatenate([add(above[:half], up), above[half:]], axis=0)
            down = jnp.concatenate([below[:half], add(below[half:], down)], axis=0)
        else:
            up, down = add(above, up), add(below, down)


def add_terms(*terms):
    return sum(t.astype(F32) for t in terms).astype(BF16)


def gather_z(piece, held):
    below, above = [piece], [piece]
    for _ in range(NZ // 2 - 1):
        below.append(shifted(below[-1], "z", NZ, 1))
        above.append(shifted(above[-1], "z", NZ, -1))
    held, _ = lax.optimization_barrier((held, above[HOLD]))
    half = piece.shape[0] // 2
    far = [shifted(below[-1][:half], "z", NZ, 1), shifted(above[-1][half:], "z", NZ, -1)]
    return jnp.stack([*above, jnp.concatenate(far, axis=0), *below[:0:-1]]), held


def per_device(queries, cotangent, passages, w_kv, neighbour_ids, passage_slot):
    enc_count, near_len, part_width = passages.shape
    seq_tokens, part_cols = queries.shape
    groups = seq_tokens // GROUP
    heads = part_cols // HEAD_DIM
    my_y = lax.axis_index("y")
    here = jnp.stack([lax.axis_index(axis) for axis in ("z", "x", "c")])
    head_ranges = ((0, FIRST_HEADS), (FIRST_HEADS, heads))
    ids = neighbour_ids.reshape(-1)
    queries = queries.reshape(groups, GROUP, part_cols)
    cotangent = cotangent.reshape(groups, GROUP, part_cols)

    piece = passages.reshape(enc_count * near_len, part_width)
    half = piece.shape[0] // 2
    [queued] = queue_groups(ids, passage_slot, queries, cotangent)
    below, above = shifted(piece, "y", NY, 1), shifted(piece, "y", NY, -1)
    visit = lax.all_to_all(queued, LAYER, split_axis=0, concat_axis=0, tiled=True)
    far = (shifted(below[:half], "y", NY, 1), shifted(above[half:], "y", NY, -1))

    encoded = jnp.zeros((enc_count * near_len, NY * part_width), BF16)
    for k, at, part in ((0, 0, piece), (1, 0, above), (3, 0, below), (2, 0, far[0]), (2, half, far[1])):
        encoded = lax.dynamic_update_slice(encoded, part, (at, ((my_y + k) % NY) * part_width))
    kv_here = jnp.einsum("nd,dkw->knw", encoded, w_kv, preferred_element_type=F32).astype(BF16)
    kv_here, later_w = lax.optimization_barrier((kv_here, w_kv))
    later_ids, _, _ = lax.optimization_barrier((ids, queued, below))
    same, other = queue_groups(later_ids, passage_slot, queries, cotangent, here)
    other = shifted(other, "c", NC, 1)
    pairs = [jnp.stack([same[k], other[k]]) for k in range(NX)]
    kv, held = gather_z(kv_here, pairs[1:])
    rest = [pairs[0]] + [shifted(pair, "x", NX, k) for k, pair in enumerate(held, 1)]
    weights = [
        lax.dynamic_slice_in_dim(later_w, ((my_y + k) % NY) * part_width, part_width, axis=0)
        for k in range(NY)
    ]

    visit, kv, weights = lax.optimization_barrier((visit, kv, weights))
    place = visit[:, 2 * NZ * GROUP + NZ :, 0].astype(jnp.int32)
    spot, at_z = place // NZ, place % NZ
    spot_x = (spot // NC - lax.axis_index("x")) % NX
    spot_c = (spot % NC) ^ lax.axis_index("c")
    partner = ((spot_c * NX + spot_x) * NZ + at_z).reshape(-1)
    partials = []
    for head_range in head_ranges:
        if partials:
            rest, _ = lax.optimization_barrier((rest, partials[0][0]))
        own = partial_stats(here, [visit, *rest, kv] if partials else [visit, kv], head_range)
        same_core = jnp.stack([own] + [shifted(own, "x", NX, -k) for k in range(1, NX)])
        partials.append([own, same_core, shifted(same_core, "c", NC, 1)])

    def z_terms(*offsets, after=()):
        at, _ = lax.optimization_barrier((here, after))
        return visit_grads(offsets, at, partner, [visit, *rest, kv], partials, head_ranges)

    up, down = z_terms(4)
    up, down = shifted(up, "z", NZ, 1), shifted(down, "z", NZ, -1)
    ups, downs = [up[0], up[1]], [down[0], down[1]]
    for offsets in ((3, 5), (2, 6), (1, 7, 0)):
        terms = z_terms(*offsets, after=(ups, downs) if offsets[0] < 3 else ())
        if offsets[0] < 3:
            ups = [shifted(up, "z", NZ, 1) for up in ups]
            downs = [shifted(down, "z", NZ, -1) for down in downs]
        for slot in range(ENC):
            above, below = terms[slot], terms[ENC + slot]
            if offsets[0] == 3:
                ups[slot] = jnp.stack([add_terms(above[0], ups[slot]), above[1]])
                downs[slot] = jnp.stack([below[0], add_terms(below[1], downs[slot])])
            else:
                ups[slot] = add_terms(above, ups[slot])
                downs[slot] = add_terms(below, downs[slot])

    grads = []
    for slot in range(ENC):
        up, down = shifted(ups[slot], "z", NZ, 1), shifted(downs[slot], "z", NZ, -1)
        grads.append(add_terms(terms[2 * ENC + slot], up, down))
    grad_kv = jnp.concatenate(grads, axis=1)

    def y_term(k):
        return jnp.einsum(
            "knw,dkw->nd", grad_kv, weights[k], preferred_element_type=F32
        ).astype(BF16)

    out = ring_sum(y_term, "y", NY, add_terms)
    return out.reshape(enc_count, near_len, part_width)


def solution(mesh):
    fine = Mesh(mesh.devices.reshape(NZ, NX, NC, NY), ("z", "x", "c", "y"))
    dp = ("z", "x", "c")
    placed = (
        P(dp, "y"),
        P(dp, "y"),
        P(dp, None, "y"),
        P(None, None, "y"),
        P(dp, None, None),
        P(),
    )
    return jax.shard_map(
        per_device, mesh=fine, in_specs=placed, out_specs=P(dp, None, "y"), check_vma=False
    )
```

```python
import math

import jax
import jax.numpy as jnp
from jax import lax
from jax.experimental import pallas as pl
from jax.experimental.pallas import tpu as pltpu
from jax.sharding import Mesh
from jax.sharding import PartitionSpec as P

HEAD_DIM = 128
GROUP = 64
NZ, NX, NC, NY = 8, 4, 2, 4
NLAYER = NX * NC
ENC = 2
NEAR = 128
LAYER = ("x", "c")
HALF = NLAYER // 2
KERNEL_VMEM = 24 * 1024 * 1024
LOADS = 4
AHEAD = 2
HOLD = 2
FIRST_HEADS = 3
SPLIT = FIRST_HEADS * HEAD_DIM
META = 2 * NZ
BF16 = jnp.bfloat16
F32 = jnp.float32
NT = (((1,), (1,)), ((), ()))
NN = (((1,), (0,)), ((), ()))
SCALE = 1.0 / math.sqrt(HEAD_DIM)
SMEM_WHOLE = pl.BlockSpec(memory_space=pltpu.SMEM)
VMEM_WHOLE = pl.BlockSpec(memory_space=pltpu.VMEM)
ANY_WHOLE = pl.BlockSpec(memory_space=pl.ANY)


def queue_kernel(ids, slot_of, q_hbm, cot_hbm, *refs, with_meta):
    if with_meta:
        out_hbm, q_ref, cot_ref, meta_f32, meta_ref, load, store, meta_sem = refs
        first = 0
    else:
        here, same_hbm, other_hbm, q_ref, cot_ref, load, store = refs
        first = SPLIT
    groups, _, width = q_ref.shape
    part = groups // LOADS

    def loads(at):
        rows, cols = pl.ds(at * part, part), pl.ds(first, width)
        return (
            pltpu.make_async_copy(q_hbm.at[rows, :, cols], q_ref.at[rows], load.at[0, at]),
            pltpu.make_async_copy(cot_hbm.at[rows, :, cols], cot_ref.at[rows], load.at[1, at]),
        )

    def stores(ref, target, dest, z):
        for kind, source in enumerate((q_ref, cot_ref)):
            rows = pl.ds(pl.multiple_of((kind * NZ + z) * GROUP, GROUP), GROUP)
            yield pltpu.make_async_copy(
                source.at[ref // 2], target.at[dest, rows], store.at[kind, ref]
            )

    for at in range(LOADS):
        for copy in loads(at):
            copy.start()

    if with_meta:

        def place(ref, carry):
            slot = slot_of[ids[ref]]
            owner = slot // ENC
            partner = slot_of[ids[ref + 1 - 2 * (ref % 2)]] // ENC
            row = (owner % NLAYER) * META + owner // NLAYER
            where = (partner % NLAYER) * NZ + partner // NLAYER
            meta_f32[pl.ds(row, 1), :] = jnp.full((1, HEAD_DIM), slot % ENC, jnp.int32).astype(F32)
            meta_f32[pl.ds(row + NZ, 1), :] = jnp.full((1, HEAD_DIM), where, jnp.int32).astype(F32)
            return carry

        lax.fori_loop(0, 2 * groups, place, 0)
        meta = meta_f32[...].astype(BF16).reshape(NLAYER, META, HEAD_DIM)
        for at in range(width // HEAD_DIM):
            meta_ref[:, :, at * HEAD_DIM : (at + 1) * HEAD_DIM] = meta
        meta_rows = pl.ds(2 * NZ * GROUP, META)
        meta_out = pltpu.make_async_copy(meta_ref, out_hbm.at[:, meta_rows], meta_sem)
        meta_out.start()

    def send(ref, carry):
        owner = slot_of[ids[ref]] // ENC
        dest, z = owner % NLAYER, owner // NLAYER
        if with_meta:
            for copy in stores(ref, out_hbm, dest, z):
                copy.start()
            return carry
        up = (dest // NC - here[1] + NX) % NX
        own_core = dest % NC == here[2]

        @pl.when(own_core)
        def _():
            for copy in stores(ref, same_hbm, up, z):
                copy.start()

        @pl.when(jnp.logical_not(own_core))
        def _():
            for copy in stores(ref, other_hbm, up, z):
                copy.start()

        return carry

    def finish(ref, carry):
        for copy in stores(ref, out_hbm if with_meta else same_hbm, 0, 0):
            copy.wait()
        return carry

    for at in range(LOADS):
        for copy in loads(at):
            copy.wait()
        lax.fori_loop(2 * part * at, 2 * part * (at + 1), send, 0)
    lax.fori_loop(0, 2 * groups, finish, 0)
    if with_meta:
        meta_out.wait()


def queue_groups(ids, slot_of, queries, cotangent, here=None):
    with_meta = here is None
    extra = [] if with_meta else [here]
    groups, _, width = queries.shape
    width = SPLIT if with_meta else width - SPLIT
    rows = 2 * NZ * GROUP
    rest = jax.ShapeDtypeStruct((NX, rows, width), BF16)
    block = pltpu.VMEM((groups, GROUP, width), BF16)
    sems = [pltpu.SemaphoreType.DMA((2, LOADS)), pltpu.SemaphoreType.DMA((2, 2 * groups))]
    if with_meta:
        outs = [jax.ShapeDtypeStruct((NLAYER, rows + META, width), BF16)]
        meta = [
            pltpu.VMEM((NLAYER * META, HEAD_DIM), F32),
            pltpu.VMEM((NLAYER, META, width), BF16),
        ]
        sems.append(pltpu.SemaphoreType.DMA)
    else:
        outs, meta = [rest, rest], []

    def kernel(*refs):
        queue_kernel(*refs, with_meta=with_meta)

    return pl.pallas_call(
        kernel,
        in_specs=[SMEM_WHOLE] * 2 + [ANY_WHOLE] * 2 + [SMEM_WHOLE] * len(extra),
        out_specs=[ANY_WHOLE] * len(outs),
        out_shape=outs,
        scratch_shapes=[block, block, *meta, *sems],
        compiler_params=pltpu.CompilerParams(vmem_limit_bytes=60 * 1024 * 1024),
        cost_estimate=pl.CostEstimate(
            flops=0, bytes_accessed=12 * groups * GROUP * width, transcendentals=0
        ),
        name="queue_groups",
    )(ids, slot_of, queries, cotangent, *extra)


def block_copies(sources, rows_ref, rest_ref, table_ref, sems, at, z, off, head_range):
    visit_hbm, *rest_hbm, kv_hbm = sources
    first, last = head_range[0] * HEAD_DIM, head_range[1] * HEAD_DIM
    for kind in range(2):
        rows = pl.ds(pl.multiple_of((kind * NZ + z) * GROUP, GROUP), GROUP)
        if first < SPLIT:
            yield pltpu.make_async_copy(
                visit_hbm.at[:, rows], rows_ref.at[at, kind], sems.at[at, kind]
            )
            if last > SPLIT:
                for down in range(NX):
                    yield pltpu.make_async_copy(
                        rest_hbm[down].at[:, rows],
                        rest_ref.at[down, :, at, kind],
                        sems.at[at, 3 + kind * NX + down],
                    )
    yield pltpu.make_async_copy(
        kv_hbm.at[off, :, :, pl.ds(first, last - first)], table_ref.at[at], sems.at[at, 2]
    )


def block_scratch(count, head_range):
    first, last = head_range[0] * HEAD_DIM, head_range[1] * HEAD_DIM
    rest = (NX, NC, count, 2, GROUP, last - SPLIT)
    if first >= SPLIT:
        rest = (NX, NC, 2 * NZ * GROUP, last - SPLIT)
    rest = [] if last <= SPLIT else [pltpu.VMEM(rest, BF16)]
    rows = [] if first >= SPLIT else [pltpu.VMEM((count, 2, NLAYER, GROUP, SPLIT), BF16)]
    return [
        *rows,
        *rest,
        pltpu.VMEM((count, 2, ENC * NEAR, last - first), BF16),
        pltpu.VMEM((NLAYER, META, HEAD_DIM), BF16),
        pltpu.SemaphoreType.DMA((count, 3 + 2 * NX)),
        pltpu.SemaphoreType.DMA((1 + NX,)),
    ]


def meta_copy(visit_hbm, meta_ref, sem):
    rows = pl.ds(2 * NZ * GROUP, META)
    return pltpu.make_async_copy(visit_hbm.at[:, rows, pl.ds(0, HEAD_DIM)], meta_ref, sem)


def head_operands(row_of, table_ref, meta_ref, at, z, head, half):
    cols = slice(head * HEAD_DIM, (head + 1) * HEAD_DIM)
    own_row = lax.broadcasted_iota(jnp.int32, (META, HEAD_DIM), 0) == z
    seconds, lanes = [], []
    for source in range(half * HALF, (half + 1) * HALF):
        meta = meta_ref[source].astype(F32)
        slot = jnp.sum(jnp.where(own_row, meta, 0.0), axis=0, keepdims=True)
        seconds.append(jnp.broadcast_to(slot, (GROUP, HEAD_DIM)).astype(BF16) > 0.5)
        lanes.append(slot[:, :GROUP])
    second_lanes = jnp.concatenate(lanes, axis=1) > 0.5
    rows, products = [], []
    for kind in range(2):
        plain = [row_of(kind, half * HALF + source, cols) for source in range(HALF)]
        both = lax.dot_general(
            table_ref[at, kind, :, cols],
            jnp.concatenate(plain, axis=0),
            NT,
            preferred_element_type=F32,
        )
        products.append(jnp.where(second_lanes, both[NEAR:], both[:NEAR]))
        pieces = []
        for row, second in zip(plain, seconds, strict=True):
            zero = jnp.zeros_like(row)
            pieces.append(
                jnp.concatenate([jnp.where(second, zero, row), jnp.where(second, row, zero)], axis=1)
            )
        rows.append(jnp.concatenate(pieces, axis=0))
    score, grad_prob = products[0] * SCALE, products[1]
    return score, grad_prob, rows


def rest_place(here, source):
    return (here[1] - source // NC + NX) % NX, (here[2] + source) % NC


def stats_kernel(head_range, here, *refs):
    *sources, out_ref, block_ref, table_ref, meta_ref, sems, sem = refs
    visit_hbm = sources[0]
    heads = head_range[1] - head_range[0]
    alone = head_range[0] * HEAD_DIM >= SPLIT
    rest_copies = []
    if alone:
        rest_copies = [
            pltpu.make_async_copy(sources[1 + down], block_ref.at[down], sem.at[1 + down])
            for down in range(NX)
        ]

    def copies(z):
        off = (z + NZ - here[0]) % NZ
        return block_copies(
            sources, block_ref, None, table_ref, sems, z, z, off, head_range
        )

    meta_copy(visit_hbm, meta_ref, sem.at[0]).start()
    for copy in rest_copies:
        copy.start()
    for z in range(NZ if alone else AHEAD):
        for copy in copies(z):
            copy.start()
    meta_copy(visit_hbm, meta_ref, sem.at[0]).wait()
    for copy in rest_copies:
        copy.wait()
    if alone:
        for z in range(NZ):
            for copy in copies(z):
                copy.wait()

    def one(z, carry):
        if not alone:

            @pl.when(z + AHEAD < NZ)
            def _():
                for copy in copies(z + AHEAD):
                    copy.start()

            for copy in copies(z):
                copy.wait()

        def row_of(kind, source, cols):
            if alone:
                down, core = rest_place(here, source)
                rows = pl.ds(pl.multiple_of((kind * NZ + z) * GROUP, GROUP), GROUP)
                return block_ref[down, core, rows, cols]
            return block_ref[z, kind, source, :, cols]

        for head in range(heads):
            for half in range(2):
                lanes = slice(half * HALF * GROUP, (half + 1) * HALF * GROUP)
                score, grad_prob, _ = head_operands(
                    row_of, table_ref, meta_ref, z, z, head, half
                )
                peak = jnp.max(score, axis=0, keepdims=True)
                weight = jnp.exp(score - peak)
                mass = jnp.sum(weight, axis=0, keepdims=True)
                delta = jnp.sum(weight * grad_prob, axis=0, keepdims=True) / mass
                out_ref[pl.ds(head * NZ + z, 1), lanes] = peak + jnp.log(mass)
                out_ref[pl.ds((heads + head) * NZ + z, 1), lanes] = delta
        return carry

    lax.fori_loop(0, NZ, one, 0, unroll=4 if alone else 1)


def attention_cost(blocks, heads, matmuls):
    products = blocks * heads * NLAYER * GROUP * ENC * NEAR * HEAD_DIM
    moved = blocks * heads * HEAD_DIM * 2 * (2 * NLAYER * GROUP + 2 * ENC * NEAR)
    return pl.CostEstimate(
        flops=2 * matmuls * products,
        bytes_accessed=moved,
        transcendentals=blocks * heads * NLAYER * GROUP * NEAR,
    )


def in_hbm(array):
    return pltpu.with_memory_space_constraint(array, pltpu.HBM)


def partial_stats(here, sources, head_range):
    heads = head_range[1] - head_range[0]
    return pl.pallas_call(
        lambda *refs: stats_kernel(head_range, *refs),
        in_specs=[SMEM_WHOLE] + [ANY_WHOLE] * len(sources),
        out_specs=VMEM_WHOLE,
        out_shape=jax.ShapeDtypeStruct((NZ * 2 * heads, NLAYER * GROUP), F32),
        scratch_shapes=block_scratch(NZ, head_range),
        compiler_params=pltpu.CompilerParams(vmem_limit_bytes=KERNEL_VMEM),
        cost_estimate=attention_cost(NZ, heads, 2),
        name="partial_stats",
    )(here, *(in_hbm(source) for source in sources))


def grads_kernel(head_ranges, offsets, here, partner, *refs):
    *sources, partials, out_refs, rows_ref, rest_ref, table_ref, meta_ref, sems, sem = refs
    visit_hbm = sources[0]
    all_heads = (0, head_ranges[-1][1])

    def copies(at):
        off = offsets[at]
        z = (here[0] + off) % NZ
        return block_copies(
            sources, rows_ref, rest_ref, table_ref, sems, at, z, off, all_heads
        )

    for copy in copies(0):
        copy.start()
    meta_copy(visit_hbm, meta_ref, sem.at[0]).start()
    meta_copy(visit_hbm, meta_ref, sem.at[0]).wait()
    low_lane = lax.broadcasted_iota(jnp.int32, (NZ, 2 * GROUP), 1) < GROUP
    z_row = lax.broadcasted_iota(jnp.int32, (NZ, 2 * GROUP), 0)
    for at_offset, off in enumerate(offsets):
        for copy in copies(at_offset):
            copy.wait()
        if at_offset + 1 < len(offsets):
            for copy in copies(at_offset + 1):
                copy.start()
        z = (here[0] + off) % NZ
        places = [partner[source * NZ + z] for source in range(NLAYER)]

        def other(same_ref, other_ref, row, half, places=places):
            tiles = slice(row * NZ, (row + 1) * NZ)
            pieces = []
            for pair in range(half * HALF // 2, (half + 1) * HALF // 2):
                cols = slice(pair * 2 * GROUP, (pair + 1) * 2 * GROUP)
                low, high = (
                    jnp.where(
                        z_row == where % NZ,
                        jnp.where(
                            where < NX * NZ,
                            same_ref[(where // NZ) % NX, tiles, cols],
                            other_ref[(where // NZ) % NX, tiles, cols],
                        ),
                        0.0,
                    )
                    for where in places[2 * pair : 2 * pair + 2]
                )
                pieces.append(jnp.sum(jnp.where(low_lane, low, high), axis=0, keepdims=True))
            return jnp.concatenate(pieces, axis=1)

        def row_of(kind, source, cols, at_offset=at_offset):
            if cols.start < SPLIT:
                return rows_ref[at_offset, kind, source, :, cols]
            down, core = rest_place(here, source)
            cols = slice(cols.start - SPLIT, cols.stop - SPLIT)
            return rest_ref[down, core, at_offset, kind, :, cols]

        for head in range(all_heads[1]):
            cols = slice(head * HEAD_DIM, (head + 1) * HEAD_DIM)
            chunk = 0 if head < head_ranges[0][1] else 1
            own_ref, *exchanged = partials[chunk]
            first, last = head_ranges[chunk]
            lse_at, delta_at = head - first, last - first + head - first
            grads = [None, None]
            for half in range(2):
                lanes = slice(half * HALF * GROUP, (half + 1) * HALF * GROUP)
                score, grad_prob, rows = head_operands(
                    row_of, table_ref, meta_ref, at_offset, z, head, half
                )
                lse_mine = own_ref[pl.ds(lse_at * NZ + z, 1), lanes]
                delta_mine = own_ref[pl.ds(delta_at * NZ + z, 1), lanes]
                lse_other = other(*exchanged, lse_at, half)
                delta_other = other(*exchanged, delta_at, half)
                top = jnp.maximum(lse_mine, lse_other)
                total = top + jnp.log(jnp.exp(lse_mine - top) + jnp.exp(lse_other - top))
                delta = delta_mine * jnp.exp(lse_mine - total) + delta_other * jnp.exp(
                    lse_other - total
                )
                probs = jnp.exp(score - total)
                dscore = probs * (grad_prob - delta)
                for at, weight in enumerate((dscore, probs)):
                    grad = lax.dot_general(
                        weight.astype(BF16), rows[at], NN, preferred_element_type=F32
                    )
                    grads[at] = grad if half == 0 else grads[at] + grad
            for at, grad in enumerate((grads[0] * SCALE, grads[1])):
                for slot in range(ENC):
                    part = grad[:, slot * HEAD_DIM : (slot + 1) * HEAD_DIM].astype(BF16)
                    if len(offsets) == 1:
                        out_refs[at][slot, :, cols] = part
                    else:
                        out_refs[ENC * at_offset + slot][at, :, cols] = part


def visit_grads(offsets, here, partner, sources, partials, head_ranges):
    width = head_ranges[-1][1] * HEAD_DIM
    parts = 2 * len(offsets)
    count = len(sources)
    flat = [array for chunk in partials for array in chunk]

    def kernel(here, partner, *refs):
        refs = list(refs)
        ins, refs = refs[:count], refs[count:]
        chunks, refs = refs[: len(flat)], refs[len(flat) :]
        chunks = [chunks[3 * i : 3 * i + 3] for i in range(len(head_ranges))]
        grads_kernel(head_ranges, offsets, here, partner, *ins, chunks, refs[:parts], *refs[parts:])

    return pl.pallas_call(
        kernel,
        in_specs=[SMEM_WHOLE] * 2 + [ANY_WHOLE] * count + [VMEM_WHOLE] * len(flat),
        out_specs=[VMEM_WHOLE] * parts,
        out_shape=[jax.ShapeDtypeStruct((2, NEAR, width), BF16)] * parts,
        scratch_shapes=block_scratch(len(offsets), (0, head_ranges[-1][1])),
        compiler_params=pltpu.CompilerParams(vmem_limit_bytes=KERNEL_VMEM),
        cost_estimate=attention_cost(len(offsets), width // HEAD_DIM, 4),
        name="visit_grads",
    )(here, partner, *(in_hbm(source) for source in sources), *flat)


def shifted(array, axis, size, by):
    return lax.ppermute(array, axis, [(i, (i + by) % size) for i in range(size)])


def ring_sum(term, axis, size, add):
    far = term(size // 2)
    half = far.shape[0] // 2
    up, down = far[:half], far[half:]
    for k in range(size // 2, 0, -1):
        up = shifted(up, axis, size, 1)
        down = shifted(down, axis, size, -1)
        if k == 1:
            return add(term(0), up, down)
        above, below = term(k - 1), term(size - k + 1)
        if k == size // 2:
            up = jnp.concatenate([add(above[:half], up), above[half:]], axis=0)
            down = jnp.concatenate([below[:half], add(below[half:], down)], axis=0)
        else:
            up, down = add(above, up), add(below, down)


def add_terms(*terms):
    return sum(t.astype(F32) for t in terms).astype(BF16)


def gather_z(piece, held):
    below, above = [piece], [piece]
    for _ in range(NZ // 2 - 1):
        below.append(shifted(below[-1], "z", NZ, 1))
        above.append(shifted(above[-1], "z", NZ, -1))
    held, _ = lax.optimization_barrier((held, above[HOLD]))
    half = piece.shape[0] // 2
    far = [shifted(below[-1][:half], "z", NZ, 1), shifted(above[-1][half:], "z", NZ, -1)]
    return jnp.stack([*above, jnp.concatenate(far, axis=0), *below[:0:-1]]), held


def per_device(queries, cotangent, passages, w_kv, neighbour_ids, passage_slot):
    enc_count, near_len, part_width = passages.shape
    seq_tokens, part_cols = queries.shape
    groups = seq_tokens // GROUP
    heads = part_cols // HEAD_DIM
    my_y = lax.axis_index("y")
    here = jnp.stack([lax.axis_index(axis) for axis in ("z", "x", "c")])
    head_ranges = ((0, FIRST_HEADS), (FIRST_HEADS, heads))
    ids = neighbour_ids.reshape(-1)
    queries = queries.reshape(groups, GROUP, part_cols)
    cotangent = cotangent.reshape(groups, GROUP, part_cols)

    piece = passages.reshape(enc_count * near_len, part_width)
    half = piece.shape[0] // 2
    [queued] = queue_groups(ids, passage_slot, queries, cotangent)
    below, above = shifted(piece, "y", NY, 1), shifted(piece, "y", NY, -1)
    visit = lax.all_to_all(queued, LAYER, split_axis=0, concat_axis=0, tiled=True)
    far = (shifted(below[:half], "y", NY, 1), shifted(above[half:], "y", NY, -1))

    encoded = jnp.zeros((enc_count * near_len, NY * part_width), BF16)
    for k, at, part in ((0, 0, piece), (1, 0, above), (3, 0, below), (2, 0, far[0]), (2, half, far[1])):
        encoded = lax.dynamic_update_slice(encoded, part, (at, ((my_y + k) % NY) * part_width))
    kv_here = jnp.einsum("nd,dkw->knw", encoded, w_kv, preferred_element_type=F32).astype(BF16)
    kv_here, later_w = lax.optimization_barrier((kv_here, w_kv))
    later_ids, _, _ = lax.optimization_barrier((ids, queued, below))
    same, other = queue_groups(later_ids, passage_slot, queries, cotangent, here)
    other = shifted(other, "c", NC, 1)
    pairs = [jnp.stack([same[k], other[k]]) for k in range(NX)]
    kv, held = gather_z(kv_here, pairs[1:])
    rest = [pairs[0]] + [shifted(pair, "x", NX, k) for k, pair in enumerate(held, 1)]
    weights = [
        lax.dynamic_slice_in_dim(later_w, ((my_y + k) % NY) * part_width, part_width, axis=0)
        for k in range(NY)
    ]

    visit, kv, weights = lax.optimization_barrier((visit, kv, weights))
    place = visit[:, 2 * NZ * GROUP + NZ :, 0].astype(jnp.int32)
    spot, at_z = place // NZ, place % NZ
    spot_x = (spot // NC - lax.axis_index("x")) % NX
    spot_c = (spot % NC) ^ lax.axis_index("c")
    partner = ((spot_c * NX + spot_x) * NZ + at_z).reshape(-1)
    partials = []
    for head_range in head_ranges:
        if partials:
            rest, _ = lax.optimization_barrier((rest, partials[0][0]))
        own = partial_stats(here, [visit, *rest, kv] if partials else [visit, kv], head_range)
        same_core = jnp.stack([own] + [shifted(own, "x", NX, -k) for k in range(1, NX)])
        partials.append([own, same_core, shifted(same_core, "c", NC, 1)])

    def z_terms(*offsets, after=()):
        at, _ = lax.optimization_barrier((here, after))
        return visit_grads(offsets, at, partner, [visit, *rest, kv], partials, head_ranges)

    up, down = z_terms(4)
    up, down = shifted(up, "z", NZ, 1), shifted(down, "z", NZ, -1)
    ups, downs = [up[0], up[1]], [down[0], down[1]]
    for offsets in ((3, 5), (2, 6), (1, 7, 0)):
        terms = z_terms(*offsets, after=(ups, downs) if offsets[0] < 3 else ())
        if offsets[0] < 3:
            ups = [shifted(up, "z", NZ, 1) for up in ups]
            downs = [shifted(down, "z", NZ, -1) for down in downs]
        for slot in range(ENC):
            above, below = terms[slot], terms[ENC + slot]
            if offsets[0] == 3:
                ups[slot] = jnp.stack([add_terms(above[0], ups[slot]), above[1]])
                downs[slot] = jnp.stack([below[0], add_terms(below[1], downs[slot])])
            else:
                ups[slot] = add_terms(above, ups[slot])
                downs[slot] = add_terms(below, downs[slot])

    grads = []
    for slot in range(ENC):
        up, down = shifted(ups[slot], "z", NZ, 1), shifted(downs[slot], "z", NZ, -1)
        grads.append(add_terms(terms[2 * ENC + slot], up, down))
    grad_kv = jnp.concatenate(grads, axis=1)

    def y_term(k):
        return jnp.einsum(
            "knw,dkw->nd", grad_kv, weights[k], preferred_element_type=F32
        ).astype(BF16)

    out = ring_sum(y_term, "y", NY, add_terms)
    return out.reshape(enc_count, near_len, part_width)


def solution(mesh):
    fine = Mesh(mesh.devices.reshape(NZ, NX, NC, NY), ("z", "x", "c", "y"))
    dp = ("z", "x", "c")
    placed = (
        P(dp, "y"),
        P(dp, "y"),
        P(dp, None, "y"),
        P(None, None, "y"),
        P(dp, None, None),
        P(),
    )
    return jax.shard_map(
        per_device, mesh=fine, in_specs=placed, out_specs=P(dp, None, "y"), check_vma=False
    )
```
